32 devices in a mesh: ctx: 8 (over y, x, core), tp: 4 (over z).
Axes of the slice: x: 2, y: 2, z: 4, core: 2. Of those that a mesh axis runs over, the one named last changes fastest.
Arguments:
- out_grad: bfloat16 [2048, 8192], P('ctx', 'tp'), may hold values from -6 to 6
- query_rows: bfloat16 [2048, 8192], P('ctx', 'tp'), may hold values from -6 to 6
- key_rows: bfloat16 [2048, 8192], P('ctx', 'tp'), may hold values from -6 to 6
- value_rows: bfloat16 [2048, 8192], P('ctx', 'tp'), may hold values from -6 to 6
- conv_rows: bfloat16 [2048, 8192], P('ctx', 'tp'), may hold values from -6 to 6
- long_filter: float32 [768, 8192], P('ctx', 'tp'), may hold values from -0.21650635 to 0.21650635
- block_table: int32 [16], replicated, may hold values from 0 to 15, each once
Outputs:
- q_grad: bfloat16 [2048, 8192], P('ctx', 'tp')
- k_grad: bfloat16 [2048, 8192], P('ctx', 'tp')
- v_grad: bfloat16 [2048, 8192], P('ctx', 'tp')
- filter_grad: float32 [768, 8192], P('ctx', 'tp')
The draws below stay inside these ranges and needn't reach their ends.
Inputs may be any that keep to these rules, and one draw needn't show every extreme that they name: slot s, block s % 2 of the device with index s // 2 along ctx, holds sequence block block_table[s]; every block appears once.
All inputs are finite; a program needn't handle non-finite values.
Results may differ from the reference program's by a relative error of at most 0.009.
Values may be sent and summed in bfloat16 or wider, within the bound.
No kernel may reach another device: no remote copies, remote signals or barrier semaphores. Data moves between devices by JAX's collectives and lax.ppermute only.
A program may use at most 192 MiB of HBM per device.

```python
import math
import jax
import jax.numpy as jnp
from jax import lax

D = 8192
BLOCK = 128
LAG_BLOCKS = 6
SEQ = 2048
N_CTX = 8
N_TP = 4


def draw_long_filter(key, part):
    key = jax.random.fold_in(key, 11)
    noise_key, reach_key = jax.random.split(key)
    lag_total = LAG_BLOCKS * BLOCK
    position = jnp.arange(lag_total, dtype=jnp.float32)[:, None]
    amplitude = lag_total ** (-0.5)
    noise = jnp.clip(jax.random.normal(noise_key, (lag_total, D), jnp.float32), -6.0, 6.0)
    reach = jnp.exp(jax.random.uniform(reach_key, (1, D), jnp.float32, math.log(30.0), math.log(4.0 * lag_total)))
    return noise * jnp.exp(-position / reach) * amplitude


def steps_of(own_key, extent, pieces, smallest, high):
    factor_of, own = 1.0, jax.random.fold_in(own_key, 6)
    for dim, blocks in pieces:
        draws = jnp.exp(jax.random.uniform(jax.random.fold_in(own, dim), (blocks,), jnp.float32, smallest / len(pieces), high / len(pieces)))
        factor_of = factor_of * jnp.repeat(draws, extent[dim] // blocks).reshape([-1 if axis == dim else 1 for axis in range(len(extent))])
    return factor_of


def normal_values(key, shape, width, most, pieces=(), kind=jnp.bfloat16):
    entries = width * jax.random.normal(key, shape, jnp.float32)
    if pieces:
        entries = entries * steps_of(key, shape, pieces, -0.22, 0.18)
    return jnp.clip(entries, -most, most).astype(kind)


def setup_inputs(seed: int = 0) -> dict:
    streams_of = jax.random.split(jax.random.key(seed), 8)
    out_grad = normal_values(streams_of[0], (SEQ, D), 1.0, 6.0, ((0, 8), (1, 4)))
    query_rows = normal_values(streams_of[1], (SEQ, D), 1.0, 6.0, ((0, 8), (1, 4)))
    key_rows = normal_values(streams_of[2], (SEQ, D), 1.0, 6.0, ((0, 8), (1, 4)))
    value_rows = normal_values(streams_of[3], (SEQ, D), 1.0, 6.0, ((0, 8), (1, 4)))
    conv_rows = normal_values(streams_of[4], (SEQ, D), 1.0, 6.0, ((0, 8), (1, 4)))
    long_filter = draw_long_filter(jax.random.fold_in(streams_of[7], 71), 0)
    block_table = jax.random.permutation(streams_of[6], 2 * N_CTX).astype(jnp.int32)
    return {"out_grad": out_grad, "query_rows": query_rows, "key_rows": key_rows, "value_rows": value_rows, "conv_rows": conv_rows, "long_filter": long_filter, "block_table": block_table}


def to_sequence(slot_rows, block_table):
    columns = slot_rows.shape[1]
    blocks = slot_rows.reshape(2 * N_CTX, BLOCK, columns)
    ordered = jnp.zeros_like(blocks).at[block_table].set(blocks)
    return ordered.reshape(2 * N_CTX * BLOCK, columns)


def to_slots(seq_rows, block_table):
    columns = seq_rows.shape[1]
    blocks = seq_rows.reshape(2 * N_CTX, BLOCK, columns)
    return blocks[block_table].reshape(2 * N_CTX * BLOCK, columns)


def correlate(leading, trailing, lag_count):
    length = 2 * (leading.shape[0] + trailing.shape[0])
    spectrum = jnp.conj(jnp.fft.rfft(leading, n=length, axis=0)) * jnp.fft.rfft(trailing, n=length, axis=0)
    return jnp.fft.irfft(spectrum, n=length, axis=0)[:lag_count]


def group_grads(member):
    w_rows, u_rows, taps = member
    factor = (2.0 * N_CTX * BLOCK) ** -0.5
    seq_grad = correlate(taps, w_rows, 2 * N_CTX * BLOCK)
    filter_raw = correlate(u_rows, w_rows, LAG_BLOCKS * BLOCK) * factor
    return seq_grad, filter_raw


def rounded(values):
    low = lax.optimization_barrier(values.astype(jnp.bfloat16))
    return low.astype(jnp.float32)


def reference(out_grad, query_rows, key_rows, value_rows, conv_rows, long_filter, block_table):
    groups = N_TP
    col_group = D // N_TP

    def split_cols(rows):
        return rows.reshape(rows.shape[0], groups, col_group).transpose(1, 0, 2)

    def join_cols(stacked):
        return stacked.transpose(1, 0, 2).reshape(stacked.shape[1], groups * col_group)

    grad_f = out_grad.astype(jnp.float32)
    key_f = key_rows.astype(jnp.float32)
    value_f = value_rows.astype(jnp.float32)
    q_grad = (grad_f * conv_rows.astype(jnp.float32)).astype(jnp.bfloat16)
    weighted = rounded(grad_f * query_rows.astype(jnp.float32))
    product = rounded(key_f * value_f)
    w_seq = to_sequence(weighted, block_table)
    u_seq = to_sequence(product, block_table)
    seq_grad, filter_raw = lax.map(group_grads, (split_cols(w_seq), split_cols(u_seq), split_cols(long_filter)))
    seq_grad = to_slots(join_cols(seq_grad), block_table)
    filter_raw = join_cols(filter_raw)
    k_grad = (seq_grad * value_f).astype(jnp.bfloat16)
    v_grad = (seq_grad * key_f).astype(jnp.bfloat16)
    return q_grad, k_grad, v_grad, filter_raw
```

```python
import functools
import math

import jax
import jax.numpy as jnp
import ml_dtypes
import numpy as np
from jax import lax
from jax.experimental import pallas as pl
from jax.experimental.pallas import tpu as pltpu
from jax.sharding import PartitionSpec as P

BLOCK = 128
LAG_BLOCKS = 6
SPAN = 2 * BLOCK
LAG_SPANS = LAG_BLOCKS * BLOCK // SPAN
LANES = 128
VMEM_BYTES = 32 * 2**20


def step_orders(ranks):
    if ranks != 8:
        return [list(range(ranks))] * 3
    return [4, 1, 2, 6, 7, 5, 3, 0], [7, 5, 3, 1, 4, 2, 6, 0], [4, 2, 5, 3, 1, 6, 7, 0]


def early_steps(ranks):
    return [6, 7] if ranks == 8 else []


def starts_after(ranks):
    return {4: 8 + 6, 2: 8 + 7, 6: 4, 7: 2} if ranks == 8 else {}


def transform_tables():
    order = np.concatenate([np.arange(0, SPAN, 2), np.arange(1, SPAN, 2)])
    angles = np.outer(order + 0.5, np.arange(SPAN)) * (math.pi / SPAN)
    forward = np.concatenate([np.cos(angles), -np.sin(angles)], 0)
    inverse = forward.T / SPAN
    return forward.astype(ml_dtypes.bfloat16), inverse.astype(ml_dtypes.bfloat16)


def swapped(device, step):
    return jnp.bitwise_xor(device, step)


def prepare_kernel(*refs, ranks, count, after):
    sources, refs = refs[:count], refs[count + after :]
    targets, rest = refs[:ranks], refs[ranks:]
    slabs, in_sems = rest[:count], rest[count]
    rows, half = slabs[0].shape[1:]
    width = 2 * half // ranks
    device = lax.axis_index("ctx")
    upper = lax.shift_right_logical(device, int(math.log2(ranks)) - 1)
    loads = []
    for group in range(2):
        columns = pl.ds(pl.multiple_of(swapped(upper, group) * half, LANES), half)
        loads.append(
            [
                pltpu.make_async_copy(source.at[:, columns], slab.at[group], in_sems.at[group, at])
                for at, (source, slab) in enumerate(zip(sources, slabs))
            ]
        )
        for load in loads[group]:
            load.start()
    for step in range(ranks):
        group, inner = divmod(step, ranks // 2)
        if inner == 0:
            for load in loads[group]:
                load.wait()
        column = jnp.bitwise_and(swapped(device, inner), ranks // 2 - 1) * width
        columns = pl.ds(pl.multiple_of(column, LANES), width)
        targets[step][:rows] = slabs[0][group, :, columns] * slabs[1][group, :, columns]
        if count == 3:
            targets[step][rows:] = slabs[2][group, :, columns].astype(jnp.bfloat16)


def prepare(arrays, ranks, after=()):
    rows, channels = arrays[0].shape
    width = channels // ranks
    out_rows = rows + sum(a.shape[0] for a in arrays[2:])
    if width % LANES:
        left, right, *below = [a.astype(jnp.float32) for a in arrays]
        packed = jnp.concatenate([left * right, *below], 0).astype(jnp.bfloat16)
        packed = packed.reshape(out_rows, ranks, width).transpose(1, 0, 2)
        device = lax.axis_index("ctx")
        return [lax.dynamic_index_in_dim(packed, device ^ m, 0, False) for m in range(ranks)]
    half = channels // 2
    slabs = [pltpu.VMEM((2, a.shape[0], half), a.dtype) for a in arrays]
    return pl.pallas_call(
        functools.partial(prepare_kernel, ranks=ranks, count=len(arrays), after=len(after)),
        in_specs=[pl.BlockSpec(memory_space=pltpu.HBM)] * len(arrays)
        + [pl.BlockSpec(memory_space=pl.ANY)] * len(after),
        out_specs=[pl.BlockSpec(memory_space=pltpu.VMEM)] * ranks,
        out_shape=[jax.ShapeDtypeStruct((out_rows, width), jnp.bfloat16)] * ranks,
        scratch_shapes=slabs + [pltpu.SemaphoreType.DMA((2, len(arrays)))],
        compiler_params=pltpu.CompilerParams(vmem_limit_bytes=VMEM_BYTES),
        cost_estimate=pl.CostEstimate(
            flops=rows * channels, bytes_accessed=8 * out_rows * channels, transcendentals=0
        ),
    )(*(pltpu.with_memory_space_constraint(a, pltpu.HBM) for a in arrays), *after)


class Spans:
    def __init__(self, table_ref, slot_ref, ranks):
        self.slot_ref = slot_ref
        for slot in range(2 * ranks):
            slot_ref[table_ref[slot]] = slot

    def place(self, block):
        slot = self.slot_ref[block]
        start = pl.multiple_of(jnp.bitwise_and(slot, 1) * BLOCK, BLOCK)
        return lax.shift_right_logical(slot, 1), start

    def read(self, ref, span):
        halves = []
        for block in (2 * span, 2 * span + 1):
            source, start = self.place(block)
            halves.append(ref[source, pl.ds(start, BLOCK), :])
        return jnp.concatenate(halves, 0)

    def write(self, ref, span, values):
        for half in range(2):
            source, start = self.place(2 * span + half)
            ref[source, pl.ds(start, BLOCK), :] = values[half * BLOCK : (half + 1) * BLOCK]


def gather_pieces(pieces, recv_ref, message):
    device = lax.axis_index("ctx")
    for step, piece in zip(step_orders(len(pieces))[message], pieces):
        recv_ref[swapped(device, step)] = piece[...]


def added(total, left, right):
    term_real = left[0] * right[0] + left[1] * right[1]
    term_imag = left[0] * right[1] - left[1] * right[0]
    return (term_real, term_imag) if total is None else (total[0] + term_real, total[1] + term_imag)


def settle(ref, index, place, sign, here, beyond):
    if beyond is not None:
        if sign > 0:
            here = here[0] + beyond[1], here[1] - beyond[0]
        else:
            here = here[0] - beyond[1], here[1] + beyond[0]
    store(ref, index, place, here)


def load(ref, index, place):
    real, imag, lanes = place
    return ref[index, real, lanes], ref[index, imag, lanes]


def store(ref, index, place, values):
    real, imag, lanes = place
    ref[index, real, lanes], ref[index, imag, lanes] = values


def each_place(width, combine):
    lane_size = LANES if width % LANES == 0 else width
    for sign in (1, -1):

        def step(index, carry, sign=sign):
            row = index * 8 if sign > 0 else index * 8 + SPAN // 2
            real = pl.ds(pl.multiple_of(row, 8), 8)
            imag = pl.ds(pl.multiple_of(row + SPAN, 8), 8)
            for lane in range(0, width, lane_size):
                combine((real, imag, slice(lane, lane + lane_size)), sign)
            return carry

        lax.fori_loop(0, SPAN // 16, step, 0)


def invert(inverse, spectrum):
    return jnp.dot(inverse, spectrum.astype(jnp.bfloat16), preferred_element_type=jnp.float32)


def weighted_kernel(table_ref, forward_ref, inverse_ref, *refs):
    slot_ref, recv_ref, f_ref, s_ref = refs[-4:]
    ranks, _, width = recv_ref.shape
    pieces, (seq_ref, w_ref, *early_refs) = refs[:ranks], refs[ranks:-4]
    spans = Spans(table_ref, slot_ref, ranks)
    gather_pieces(pieces, recv_ref, 0)
    forward = forward_ref[...]
    taps = jnp.concatenate([recv_ref[source, SPAN:, :] for source in range(ranks)], 0)
    for lag in range(LAG_SPANS):
        rows = taps[lag * SPAN : (lag + 1) * SPAN]
        f_ref[lag] = jnp.dot(forward, rows, preferred_element_type=jnp.float32)
    for span in range(ranks):
        w_ref[span] = jnp.dot(forward, spans.read(recv_ref, span), preferred_element_type=jnp.float32)

    def combine(place, sign):
        filters = [load(f_ref, lag, place) for lag in range(LAG_SPANS)]
        sums = [None] * (ranks + 1)
        for span in range(ranks):
            weighted = load(w_ref, span, place)
            for lag in range(min(LAG_SPANS - 1, span) + 1):
                sums[span - lag] = added(sums[span - lag], filters[lag], weighted)
            done = span - LAG_SPANS
            if done >= 0:
                settle(s_ref, done, place, sign, sums[done], sums[done + 1])
        for span in range(max(0, ranks - LAG_SPANS), ranks):
            settle(s_ref, span, place, sign, sums[span], sums[span + 1])

    each_place(width, combine)
    inverse = inverse_ref[...]
    for span in range(ranks):
        spans.write(seq_ref, span, invert(inverse, s_ref[span]).astype(jnp.bfloat16))
    device = lax.axis_index("ctx")
    for step, early_ref in zip(early_steps(ranks), early_refs):
        early_ref[...] = seq_ref[swapped(device, step)]


def product_kernel(table_ref, forward_ref, inverse_ref, w_ref, seq_ref, *refs):
    slot_ref, recv_ref, u_ref, g_ref = refs[-4:]
    ranks, _, width = recv_ref.shape
    pieces, targets = refs[:ranks], refs[ranks:-4]
    factor = (2.0 * BLOCK * ranks) ** -0.5
    spans = Spans(table_ref, slot_ref, ranks)
    gather_pieces(pieces, recv_ref, 1)
    forward = forward_ref[...]
    for span in range(ranks):
        u_ref[span] = jnp.dot(forward, spans.read(recv_ref, span), preferred_element_type=jnp.float32)

    def combine(place, sign):
        lagged = [None] * (LAG_SPANS + 1)
        products = []
        for span in range(ranks):
            weighted = load(w_ref, span, place)
            products.append(load(u_ref, span, place))
            for lag in range(min(LAG_SPANS, span) + 1):
                lagged[lag] = added(lagged[lag], products[span - lag], weighted)
        for lag in range(LAG_SPANS):
            settle(g_ref, lag, place, sign, lagged[lag], lagged[lag + 1])

    each_place(width, combine)
    inverse = inverse_ref[...]
    lags = [(invert(inverse, g_ref[lag]) * factor).astype(jnp.bfloat16) for lag in range(LAG_SPANS)]
    lag_rows = jnp.concatenate(lags, 0)
    taps = lag_rows.shape[0] // ranks
    device = lax.axis_index("ctx")
    for source in range(ranks):
        recv_ref[source, :taps] = lag_rows[source * taps : (source + 1) * taps]
    for step, target in enumerate(targets):
        owner = swapped(device, step)
        if step not in early_steps(ranks):
            target[:SPAN] = seq_ref[owner]
        target[-taps:] = recv_ref[owner, :taps]


def spectral_call(kernel, operands, out_shape, scratch, flops, ranks):
    whole = pl.BlockSpec(memory_space=pltpu.VMEM)
    return pl.pallas_call(
        kernel,
        in_specs=[pl.BlockSpec(memory_space=pltpu.SMEM)] + [whole] * (len(operands) - 1),
        out_specs=[whole] * len(out_shape),
        out_shape=out_shape,
        scratch_shapes=[pltpu.SMEM((2 * ranks,), jnp.int32)] + scratch,
        compiler_params=pltpu.CompilerParams(vmem_limit_bytes=VMEM_BYTES),
        cost_estimate=pl.CostEstimate(
            flops=flops,
            bytes_accessed=sum(a.size * a.dtype.itemsize for a in (*operands, *out_shape)),
            transcendentals=0,
        ),
    )(*operands)


def weighted_part(received, constants):
    ranks = len(received)
    recv_rows, width = received[0].shape
    return spectral_call(
        weighted_kernel,
        (*constants, *received),
        [
            jax.ShapeDtypeStruct((ranks, SPAN, width), jnp.bfloat16),
            jax.ShapeDtypeStruct((ranks, 2 * SPAN, width), jnp.float32),
        ]
        + [jax.ShapeDtypeStruct((SPAN, width), jnp.bfloat16)] * len(early_steps(ranks)),
        [
            pltpu.VMEM((ranks, recv_rows, width), jnp.bfloat16),
            pltpu.VMEM((LAG_SPANS, 2 * SPAN, width), jnp.float32),
            pltpu.VMEM((ranks, 2 * SPAN, width), jnp.float32),
        ],
        4 * SPAN * SPAN * width * (2 * ranks + LAG_SPANS),
        ranks,
    )


def product_part(received, seq_grad, spectrum, constants):
    ranks = len(received)
    width = received[0].shape[1]
    taps = LAG_SPANS * SPAN // ranks
    early = early_steps(ranks)
    return spectral_call(
        product_kernel,
        (*constants, spectrum, seq_grad, *received),
        [
            jax.ShapeDtypeStruct((taps if step in early else SPAN + taps, width), jnp.bfloat16)
            for step in range(ranks)
        ],
        [
            pltpu.VMEM((ranks, SPAN, width), jnp.bfloat16),
            pltpu.VMEM((ranks, 2 * SPAN, width), jnp.float32),
            pltpu.VMEM((LAG_SPANS, 2 * SPAN, width), jnp.float32),
        ],
        4 * SPAN * SPAN * width * (ranks + LAG_SPANS),
        ranks,
    )


def finish_kernel(*refs, ranks, early):
    received, early_refs, refs = refs[:ranks], refs[ranks : ranks + early], refs[ranks + early :]
    key_ref, value_ref, k_ref, v_ref, filter_ref, k_slab, v_slab, lag_slab, sems = refs
    _, rows, width = k_slab.shape
    taps = lag_slab.shape[1]
    seq_refs = dict(zip(step_orders(ranks)[2], received)) | dict(zip(early_steps(ranks), early_refs))
    lag_refs = dict(zip(step_orders(ranks)[2], received))
    device = lax.axis_index("ctx")
    stores = []
    for step in range(ranks):
        columns = pl.ds(pl.multiple_of(swapped(device, step) * width, LANES), width)
        seq_grad = seq_refs[step][:rows]
        k_slab[step] = seq_grad * value_ref[:, columns]
        v_slab[step] = seq_grad * key_ref[:, columns]
        lag_slab[step] = lag_refs[step][-taps:].astype(jnp.float32)
        for at, (slab, ref) in enumerate(((k_slab, k_ref), (v_slab, v_ref), (lag_slab, filter_ref))):
            stores.append(pltpu.make_async_copy(slab.at[step], ref.at[:, columns], sems.at[step, at]))
            stores[-1].start()
    for copy in stores:
        copy.wait()


def finish(received, early, key_rows, value_rows):
    ranks = len(received)
    width = received[0].shape[1]
    rows, channels = key_rows.shape
    taps = LAG_SPANS * SPAN // ranks
    if width % LANES:
        order = step_orders(ranks)[2]
        pieces = [received[order.index(step)] for step in range(ranks)]
        for step, piece in zip(early_steps(ranks), early):
            pieces[step] = jnp.concatenate([piece, pieces[step]], 0)
        slots = swapped(lax.axis_index("ctx"), lax.iota(jnp.int32, ranks))
        flat = jnp.stack(pieces)[slots].astype(jnp.float32).transpose(1, 0, 2)
        flat = flat.reshape(rows + taps, channels)
        seq_grad = flat[:rows]
        k_grad = (seq_grad * value_rows.astype(jnp.float32)).astype(jnp.bfloat16)
        v_grad = (seq_grad * key_rows.astype(jnp.float32)).astype(jnp.bfloat16)
        return k_grad, v_grad, flat[rows:]
    return pl.pallas_call(
        functools.partial(finish_kernel, ranks=ranks, early=len(early)),
        in_specs=[pl.BlockSpec(memory_space=pltpu.VMEM)] * (ranks + len(early) + 2),
        out_specs=[pl.BlockSpec(memory_space=pltpu.HBM)] * 3,
        out_shape=[
            jax.ShapeDtypeStruct((rows, channels), jnp.bfloat16),
            jax.ShapeDtypeStruct((rows, channels), jnp.bfloat16),
            jax.ShapeDtypeStruct((taps, channels), jnp.float32),
        ],
        scratch_shapes=[pltpu.VMEM((ranks, rows, width), jnp.bfloat16)] * 2
        + [pltpu.VMEM((ranks, taps, width), jnp.float32), pltpu.SemaphoreType.DMA((ranks, 3))],
        compiler_params=pltpu.CompilerParams(vmem_limit_bytes=VMEM_BYTES),
        cost_estimate=pl.CostEstimate(
            flops=2 * rows * channels,
            bytes_accessed=channels * (10 * rows + 6 * taps),
            transcendentals=0,
        ),
    )(*received, *early, key_rows, value_rows)


def on_device(out_grad, query_rows, key_rows, value_rows, conv_rows, long_filter, block_table):
    ranks = lax.axis_size("ctx")
    constants = (block_table, *(jnp.asarray(table) for table in transform_tables()))

    def swap(piece, step):
        pairs = [(rank, rank ^ step) for rank in range(ranks)]
        return lax.ppermute(piece, "ctx", pairs) if step else piece

    def exchange(pieces, message):
        return [swap(pieces[step], step) for step in step_orders(ranks)[message]]

    weighted = exchange(prepare((out_grad, query_rows, long_filter), ranks), 0)
    product = exchange(prepare((key_rows, value_rows), ranks, weighted[:1]), 1)
    q_grad = (out_grad.astype(jnp.float32) * conv_rows.astype(jnp.float32)).astype(jnp.bfloat16)
    seq_grad, spectrum, *early = weighted_part(weighted, constants)
    early = [swap(piece, step) for step, piece in zip(early_steps(ranks), early)]
    pieces = list(product_part(product, seq_grad, spectrum, constants))
    order = step_orders(ranks)[2]
    returned = {step + ranks: piece for step, piece in zip(early_steps(ranks), early)}
    for step in order:
        ahead = starts_after(ranks).get(step)
        if ahead is not None:
            pieces[step], returned[ahead] = lax.optimization_barrier((pieces[step], returned[ahead]))
        returned[step] = swap(pieces[step], step)
    early = [returned[step + ranks] for step in early_steps(ranks)]
    returned = [returned[step] for step in order]
    return (q_grad, *finish(returned, early, key_rows, value_rows))


def solution(mesh):
    in_specs = (P("ctx", "tp"),) * 6 + (P(),)
    out_specs = (P("ctx", "tp"),) * 4
    return jax.shard_map(
        on_device, mesh=mesh, in_specs=in_specs, out_specs=out_specs, check_vma=False
    )
```

```python
import functools
import math

import jax
import jax.numpy as jnp
import ml_dtypes
import numpy as np
from jax import lax
from jax.experimental import pallas as pl
from jax.experimental.pallas import tpu as pltpu
from jax.sharding import PartitionSpec as P

BLOCK = 128
LAG_BLOCKS = 6
SPAN = 2 * BLOCK
LAG_SPANS = LAG_BLOCKS * BLOCK // SPAN
LANES = 128
VMEM_BYTES = 32 * 2**20


def step_orders(ranks):
    if ranks != 8:
        return [list(range(ranks))] * 3
    return [4, 2, 6, 7, 5, 3, 1, 0], [5, 3, 1, 4, 2, 6, 7, 0], [4, 2, 5, 3, 1, 6, 7, 0]


def joint_steps(ranks):
    return [5, 3, 1] if ranks == 8 else []


def early_steps(ranks):
    return [6, 7] if ranks == 8 else []


def first_steps(ranks):
    return [0, 2, 4] if ranks == 8 else []


def starts_after(ranks):
    return {4: 8 + 6, 2: 8 + 7, 1: 2, 6: 2, 7: 2} if ranks == 8 else {}


def transform_tables():
    order = np.concatenate([np.arange(0, SPAN, 2), np.arange(1, SPAN, 2)])
    angles = np.outer(order + 0.5, np.arange(SPAN)) * (math.pi / SPAN)
    forward = np.concatenate([np.cos(angles), -np.sin(angles)], 0)
    inverse = forward.T / SPAN
    return forward.astype(ml_dtypes.bfloat16), inverse.astype(ml_dtypes.bfloat16)


def swapped(device, step):
    return jnp.bitwise_xor(device, step)


def prepare_kernel(*refs, ranks, count, above):
    sources, above_refs, refs = refs[:count], refs[count : count + len(above)], refs[count + len(above) :]
    targets, rest = refs[:ranks], refs[ranks:]
    slabs, in_sems = rest[:count], rest[count]
    rows, half = slabs[0].shape[1:]
    width = 2 * half // ranks
    device = lax.axis_index("ctx")
    upper = lax.shift_right_logical(device, int(math.log2(ranks)) - 1)
    loads = []
    for group in range(2):
        columns = pl.ds(pl.multiple_of(swapped(upper, group) * half, LANES), half)
        loads.append(
            [
                pltpu.make_async_copy(source.at[:, columns], slab.at[group], in_sems.at[group, at])
                for at, (source, slab) in enumerate(zip(sources, slabs))
            ]
        )
        for load in loads[group]:
            load.start()
    for step in range(ranks):
        group, inner = divmod(step, ranks // 2)
        if inner == 0:
            for load in loads[group]:
                load.wait()
        column = jnp.bitwise_and(swapped(device, inner), ranks // 2 - 1) * width
        columns = pl.ds(pl.multiple_of(column, LANES), width)
        target = targets[step]
        if step in above:
            first = target.shape[0] - rows
            target[:first] = above_refs[above.index(step)][...]
            target = target.at[first:]
        target[:rows] = slabs[0][group, :, columns] * slabs[1][group, :, columns]
        if count == 3:
            target[rows:] = slabs[2][group, :, columns].astype(jnp.bfloat16)


def prepare(arrays, ranks, above=()):
    above = dict(above)
    rows, channels = arrays[0].shape
    width = channels // ranks
    out_rows = rows + sum(a.shape[0] for a in arrays[2:])
    if width % LANES:
        left, right, *below = [a.astype(jnp.float32) for a in arrays]
        packed = jnp.concatenate([left * right, *below], 0).astype(jnp.bfloat16)
        packed = packed.reshape(out_rows, ranks, width).transpose(1, 0, 2)
        device = lax.axis_index("ctx")
        pieces = [lax.dynamic_index_in_dim(packed, device ^ m, 0, False) for m in range(ranks)]
        return [jnp.concatenate([above[m], p], 0) if m in above else p for m, p in enumerate(pieces)]
    piece_rows = [out_rows + (above[m].shape[0] if m in above else 0) for m in range(ranks)]
    half = channels // 2
    slabs = [pltpu.VMEM((2, a.shape[0], half), a.dtype) for a in arrays]
    return pl.pallas_call(
        functools.partial(prepare_kernel, ranks=ranks, count=len(arrays), above=tuple(above)),
        in_specs=[pl.BlockSpec(memory_space=pltpu.HBM)] * len(arrays)
        + [pl.BlockSpec(memory_space=pltpu.VMEM)] * len(above),
        out_specs=[pl.BlockSpec(memory_space=pltpu.VMEM)] * ranks,
        out_shape=[jax.ShapeDtypeStruct((r, width), jnp.bfloat16) for r in piece_rows],
        scratch_shapes=slabs + [pltpu.SemaphoreType.DMA((2, len(arrays)))],
        compiler_params=pltpu.CompilerParams(vmem_limit_bytes=VMEM_BYTES),
        cost_estimate=pl.CostEstimate(
            flops=rows * channels, bytes_accessed=8 * out_rows * channels, transcendentals=0
        ),
    )(*(pltpu.with_memory_space_constraint(a, pltpu.HBM) for a in arrays), *above.values())


class Spans:
    def __init__(self, table_ref, slot_ref, ranks):
        self.slot_ref = slot_ref
        for slot in range(2 * ranks):
            slot_ref[table_ref[slot]] = slot

    def place(self, block):
        slot = self.slot_ref[block]
        start = pl.multiple_of(jnp.bitwise_and(slot, 1) * BLOCK, BLOCK)
        return lax.shift_right_logical(slot, 1), start

    def read(self, ref, span):
        halves = []
        for block in (2 * span, 2 * span + 1):
            source, start = self.place(block)
            halves.append(ref[source, pl.ds(start, BLOCK), :])
        return jnp.concatenate(halves, 0)

    def write(self, ref, span, values):
        for half in range(2):
            source, start = self.place(2 * span + half)
            ref[source, pl.ds(start, BLOCK), :] = values[half * BLOCK : (half + 1) * BLOCK]


def gather_pieces(pieces, recv_ref, message):
    device = lax.axis_index("ctx")
    rows = recv_ref.shape[1]
    for step, piece in zip(step_orders(len(pieces))[message], pieces):
        recv_ref[swapped(device, step)] = piece[-rows:] if message else piece[:rows]


def added(total, left, right):
    term_real = left[0] * right[0] + left[1] * right[1]
    term_imag = left[0] * right[1] - left[1] * right[0]
    return (term_real, term_imag) if total is None else (total[0] + term_real, total[1] + term_imag)


def settle(ref, index, place, sign, here, beyond):
    if beyond is not None:
        if sign > 0:
            here = here[0] + beyond[1], here[1] - beyond[0]
        else:
            here = here[0] - beyond[1], here[1] + beyond[0]
    store(ref, index, place, here)


def load(ref, index, place):
    real, imag, lanes = place
    return ref[index, real, lanes], ref[index, imag, lanes]


def store(ref, index, place, values):
    real, imag, lanes = place
    ref[index, real, lanes], ref[index, imag, lanes] = values


def each_place(width, combine):
    lane_size = LANES if width % LANES == 0 else width
    for sign in (1, -1):

        def step(index, carry, sign=sign):
            row = index * 8 if sign > 0 else index * 8 + SPAN // 2
            real = pl.ds(pl.multiple_of(row, 8), 8)
            imag = pl.ds(pl.multiple_of(row + SPAN, 8), 8)
            for lane in range(0, width, lane_size):
                combine((real, imag, slice(lane, lane + lane_size)), sign)
            return carry

        lax.fori_loop(0, SPAN // 16, step, 0)


def invert(inverse, spectrum):
    return jnp.dot(inverse, spectrum.astype(jnp.bfloat16), preferred_element_type=jnp.float32)


def weighted_kernel(table_ref, forward_ref, inverse_ref, *refs):
    slot_ref, recv_ref, f_ref, s_ref = refs[-4:]
    ranks, _, width = recv_ref.shape
    pieces, (seq_ref, w_ref, *early_refs) = refs[:ranks], refs[ranks:-4]
    spans = Spans(table_ref, slot_ref, ranks)
    gather_pieces(pieces, recv_ref, 0)
    forward = forward_ref[...]
    taps = jnp.concatenate([recv_ref[source, SPAN:, :] for source in range(ranks)], 0)
    for lag in range(LAG_SPANS):
        rows = taps[lag * SPAN : (lag + 1) * SPAN]
        f_ref[lag] = jnp.dot(forward, rows, preferred_element_type=jnp.float32)
    for span in range(ranks):
        w_ref[span] = jnp.dot(forward, spans.read(recv_ref, span), preferred_element_type=jnp.float32)

    def combine(place, sign):
        filters = [load(f_ref, lag, place) for lag in range(LAG_SPANS)]
        sums = [None] * (ranks + 1)
        for span in range(ranks):
            weighted = load(w_ref, span, place)
            for lag in range(min(LAG_SPANS - 1, span) + 1):
                sums[span - lag] = added(sums[span - lag], filters[lag], weighted)
            done = span - LAG_SPANS
            if done >= 0:
                settle(s_ref, done, place, sign, sums[done], sums[done + 1])
        for span in range(max(0, ranks - LAG_SPANS), ranks):
            settle(s_ref, span, place, sign, sums[span], sums[span + 1])

    each_place(width, combine)
    inverse = inverse_ref[...]
    for span in range(ranks):
        spans.write(seq_ref, span, invert(inverse, s_ref[span]).astype(jnp.bfloat16))
    device = lax.axis_index("ctx")
    for step, early_ref in zip(early_steps(ranks), early_refs):
        early_ref[...] = seq_ref[swapped(device, step)]


def product_kernel(table_ref, forward_ref, inverse_ref, w_ref, seq_ref, *refs):
    slot_ref, recv_ref, u_ref, g_ref = refs[-4:]
    ranks, _, width = recv_ref.shape
    pieces, targets = refs[:ranks], refs[ranks:-4]
    factor = (2.0 * BLOCK * ranks) ** -0.5
    spans = Spans(table_ref, slot_ref, ranks)
    gather_pieces(pieces, recv_ref, 1)
    forward = forward_ref[...]
    for span in range(ranks):
        u_ref[span] = jnp.dot(forward, spans.read(recv_ref, span), preferred_element_type=jnp.float32)

    def combine(place, sign):
        lagged = [None] * (LAG_SPANS + 1)
        products = []
        for span in range(ranks):
            weighted = load(w_ref, span, place)
            products.append(load(u_ref, span, place))
            for lag in range(min(LAG_SPANS, span) + 1):
                lagged[lag] = added(lagged[lag], products[span - lag], weighted)
        for lag in range(LAG_SPANS):
            settle(g_ref, lag, place, sign, lagged[lag], lagged[lag + 1])

    each_place(width, combine)
    inverse = inverse_ref[...]
    lags = [(invert(inverse, g_ref[lag]) * factor).astype(jnp.bfloat16) for lag in range(LAG_SPANS)]
    lag_rows = jnp.concatenate(lags, 0)
    taps = lag_rows.shape[0] // ranks
    device = lax.axis_index("ctx")
    for source in range(ranks):
        recv_ref[source, :taps] = lag_rows[source * taps : (source + 1) * taps]
    for step, target in enumerate(targets):
        owner = swapped(device, step)
        if step not in early_steps(ranks):
            target[:SPAN] = seq_ref[owner]
        target[-taps:] = recv_ref[owner, :taps]


def spectral_call(kernel, operands, out_shape, scratch, flops, ranks):
    whole = pl.BlockSpec(memory_space=pltpu.VMEM)
    return pl.pallas_call(
        kernel,
        in_specs=[pl.BlockSpec(memory_space=pltpu.SMEM)] + [whole] * (len(operands) - 1),
        out_specs=[whole] * len(out_shape),
        out_shape=out_shape,
        scratch_shapes=[pltpu.SMEM((2 * ranks,), jnp.int32)] + scratch,
        compiler_params=pltpu.CompilerParams(vmem_limit_bytes=VMEM_BYTES),
        cost_estimate=pl.CostEstimate(
            flops=flops,
            bytes_accessed=sum(a.size * a.dtype.itemsize for a in (*operands, *out_shape)),
            transcendentals=0,
        ),
    )(*operands)


def weighted_part(received, constants):
    ranks = len(received)
    width = received[0].shape[1]
    recv_rows = SPAN + LAG_SPANS * SPAN // ranks
    return spectral_call(
        weighted_kernel,
        (*constants, *received),
        [
            jax.ShapeDtypeStruct((ranks, SPAN, width), jnp.bfloat16),
            jax.ShapeDtypeStruct((ranks, 2 * SPAN, width), jnp.float32),
        ]
        + [jax.ShapeDtypeStruct((SPAN, width), jnp.bfloat16)] * len(early_steps(ranks)),
        [
            pltpu.VMEM((ranks, recv_rows, width), jnp.bfloat16),
            pltpu.VMEM((LAG_SPANS, 2 * SPAN, width), jnp.float32),
            pltpu.VMEM((ranks, 2 * SPAN, width), jnp.float32),
        ],
        4 * SPAN * SPAN * width * (2 * ranks + LAG_SPANS),
        ranks,
    )


def product_part(received, seq_grad, spectrum, constants):
    ranks = len(received)
    width = received[0].shape[1]
    taps = LAG_SPANS * SPAN // ranks
    early = early_steps(ranks)
    return spectral_call(
        product_kernel,
        (*constants, spectrum, seq_grad, *received),
        [
            jax.ShapeDtypeStruct((taps if step in early else SPAN + taps, width), jnp.bfloat16)
            for step in range(ranks)
        ],
        [
            pltpu.VMEM((ranks, SPAN, width), jnp.bfloat16),
            pltpu.VMEM((ranks, 2 * SPAN, width), jnp.float32),
            pltpu.VMEM((LAG_SPANS, 2 * SPAN, width), jnp.float32),
        ],
        4 * SPAN * SPAN * width * (ranks + LAG_SPANS),
        ranks,
    )


def finish_kernel(*refs, steps):
    pieces, refs = refs[: len(steps)], refs[len(steps) :]
    (key_ref, value_ref), (k_ref, v_ref, filter_ref, k_slab, v_slab, lag_slab, sems) = refs[:2], refs[-7:]
    _, rows, width = k_slab.shape
    taps = lag_slab.shape[1]
    device = lax.axis_index("ctx")
    stores = []
    for at, (step, piece) in enumerate(zip(steps, pieces)):
        columns = pl.ds(pl.multiple_of(swapped(device, step) * width, LANES), width)
        results = []
        if piece.shape[0] >= rows:
            seq_grad = piece[:rows]
            k_slab[at] = seq_grad * value_ref[:, columns]
            v_slab[at] = seq_grad * key_ref[:, columns]
            results += [(k_slab, k_ref), (v_slab, v_ref)]
        if piece.shape[0] != rows:
            lag_slab[at] = piece[-taps:].astype(jnp.float32)
            results.append((lag_slab, filter_ref))
        for sem, (slab, ref) in enumerate(results):
            stores.append(pltpu.make_async_copy(slab.at[at], ref.at[:, columns], sems.at[at, sem]))
            stores[-1].start()
    for copy in stores:
        copy.wait()


def finish_some(pieces, key_rows, value_rows, ranks, partial):
    steps = [step for step, _ in pieces]
    rows, channels = key_rows.shape
    width = channels // ranks
    taps = LAG_SPANS * SPAN // ranks
    return pl.pallas_call(
        functools.partial(finish_kernel, steps=steps),
        in_specs=[pl.BlockSpec(memory_space=pltpu.VMEM)] * (len(pieces) + 2)
        + [pl.BlockSpec(memory_space=pltpu.HBM)] * len(partial),
        out_specs=[pl.BlockSpec(memory_space=pltpu.HBM)] * 3,
        out_shape=[
            jax.ShapeDtypeStruct((rows, channels), jnp.bfloat16),
            jax.ShapeDtypeStruct((rows, channels), jnp.bfloat16),
            jax.ShapeDtypeStruct((taps, channels), jnp.float32),
        ],
        scratch_shapes=[pltpu.VMEM((len(pieces), rows, width), jnp.bfloat16)] * 2
        + [
            pltpu.VMEM((len(pieces), taps, width), jnp.float32),
            pltpu.SemaphoreType.DMA((len(pieces), 3)),
        ],
        input_output_aliases={len(pieces) + 2 + at: at for at in range(len(partial))},
        compiler_params=pltpu.CompilerParams(vmem_limit_bytes=VMEM_BYTES),
        cost_estimate=pl.CostEstimate(
            flops=2 * rows * width * len(pieces),
            bytes_accessed=width * len(pieces) * (10 * rows + 6 * taps),
            transcendentals=0,
        ),
    )(*(piece for _, piece in pieces), key_rows, value_rows, *partial)


def finish(returned, early, key_rows, value_rows):
    ranks = len(returned)
    width = returned[0].shape[1]
    rows, channels = key_rows.shape
    if width % LANES:
        pieces = [returned[step] for step in range(ranks)]
        for step, piece in early.items():
            pieces[step] = jnp.concatenate([piece, pieces[step]], 0)
        slots = swapped(lax.axis_index("ctx"), lax.iota(jnp.int32, ranks))
        flat = jnp.stack(pieces)[slots].astype(jnp.float32).transpose(1, 0, 2)
        flat = flat.reshape(-1, channels)
        seq_grad = flat[:rows]
        k_grad = (seq_grad * value_rows.astype(jnp.float32)).astype(jnp.bfloat16)
        v_grad = (seq_grad * key_rows.astype(jnp.float32)).astype(jnp.bfloat16)
        return k_grad, v_grad, flat[rows:]
    order = step_orders(ranks)[2]
    first = first_steps(ranks)
    outputs = ()
    if first:
        pieces = [(step, returned[step]) for step in order if step in first] + list(early.items())
        outputs = finish_some(pieces, key_rows, value_rows, ranks, outputs)
    pieces = [(step, returned[step]) for step in order if step not in first]
    return finish_some(pieces, key_rows, value_rows, ranks, outputs)


def on_device(out_grad, query_rows, key_rows, value_rows, conv_rows, long_filter, block_table):
    ranks = lax.axis_size("ctx")
    constants = (block_table, *(jnp.asarray(table) for table in transform_tables()))

    def swap(piece, step):
        pairs = [(rank, rank ^ step) for rank in range(ranks)]
        return lax.ppermute(piece, "ctx", pairs) if step else piece

    def exchange(pieces):
        return {step: swap(piece, step) for step, piece in pieces.items()}

    def ordered(pieces, message):
        return [pieces[step] for step in step_orders(ranks)[message]]

    joint = joint_steps(ranks)
    pieces = prepare((out_grad, query_rows, long_filter), ranks)
    weighted = exchange({step: pieces[step] for step in range(ranks) if step not in joint})
    pieces = prepare((key_rows, value_rows), ranks, {step: pieces[step] for step in joint})
    product = exchange(dict(enumerate(pieces)))
    weighted |= {step: product[step] for step in joint}
    q_grad = (out_grad.astype(jnp.float32) * conv_rows.astype(jnp.float32)).astype(jnp.bfloat16)
    seq_grad, spectrum, *early = weighted_part(ordered(weighted, 0), constants)
    early = [swap(piece, step) for step, piece in zip(early_steps(ranks), early)]
    pieces = product_part(ordered(product, 1), seq_grad, spectrum, constants)
    pieces = list(pieces)
    returned = {step + ranks: piece for step, piece in zip(early_steps(ranks), early)}
    for step in step_orders(ranks)[2]:
        ahead = starts_after(ranks).get(step)
        if ahead is not None:
            pieces[step], returned[ahead] = lax.optimization_barrier((pieces[step], returned[ahead]))
        returned[step] = swap(pieces[step], step)
    early = {step: returned.pop(step + ranks) for step in early_steps(ranks)}
    return (q_grad, *finish(returned, early, key_rows, value_rows))


def solution(mesh):
    in_specs = (P("ctx", "tp"),) * 6 + (P(),)
    out_specs = (P("ctx", "tp"),) * 4
    return jax.shard_map(
        on_device, mesh=mesh, in_specs=in_specs, out_specs=out_specs, check_vma=False
    )
```

```python
import functools
import math

import jax
import jax.numpy as jnp
import ml_dtypes
import numpy as np
from jax import lax
from jax.experimental import pallas as pl
from jax.experimental.pallas import tpu as pltpu
from jax.sharding import PartitionSpec as P

BLOCK = 128
LAG_BLOCKS = 6
SPAN = 2 * BLOCK
LAG_SPANS = LAG_BLOCKS * BLOCK // SPAN
LANES = 128
JOINT_AHEAD = {6: 1}
VMEM_BYTES = 32 * 2**20


def step_orders(ranks):
    if ranks != 8:
        return [list(range(ranks))] * 3
    return [4, 2, 6, 7, 5, 3, 1, 0], [5, 3, 1, 4, 2, 6, 7, 0], [4, 2, 5, 3, 1, 6, 7, 0]


def joint_steps(ranks):
    return [5, 3, 1] if ranks == 8 else []


def early_steps(ranks):
    return [6, 7] if ranks == 8 else []


def first_steps(ranks):
    return [0, 2, 4] if ranks == 8 else []


def starts_after(ranks):
    return {4: 8 + 6, 2: 8 + 7, 1: 2, 6: 2, 7: 2} if ranks == 8 else {}


def transform_tables():
    order = np.concatenate([np.arange(0, SPAN, 2), np.arange(1, SPAN, 2)])
    angles = np.outer(order + 0.5, np.arange(SPAN)) * (math.pi / SPAN)
    forward = np.concatenate([np.cos(angles), -np.sin(angles)], 0)
    inverse = forward.T / SPAN
    return forward.astype(ml_dtypes.bfloat16), inverse.astype(ml_dtypes.bfloat16)


def swapped(device, step):
    return jnp.bitwise_xor(device, step)


def prepare_kernel(*refs, ranks, count, above):
    sources, above_refs, refs = refs[:count], refs[count : count + len(above)], refs[count + len(above) :]
    targets, rest = refs[:ranks], refs[ranks:]
    slabs, in_sems = rest[:count], rest[count]
    rows, half = slabs[0].shape[1:]
    width = 2 * half // ranks
    device = lax.axis_index("ctx")
    upper = lax.shift_right_logical(device, int(math.log2(ranks)) - 1)
    loads = []
    for group in range(2):
        columns = pl.ds(pl.multiple_of(swapped(upper, group) * half, LANES), half)
        loads.append(
            [
                pltpu.make_async_copy(source.at[:, columns], slab.at[group], in_sems.at[group, at])
                for at, (source, slab) in enumerate(zip(sources, slabs))
            ]
        )
        for load in loads[group]:
            load.start()
    for step in range(ranks):
        group, inner = divmod(step, ranks // 2)
        if inner == 0:
            for load in loads[group]:
                load.wait()
        column = jnp.bitwise_and(swapped(device, inner), ranks // 2 - 1) * width
        columns = pl.ds(pl.multiple_of(column, LANES), width)
        target = targets[step]
        if step in above:
            first = target.shape[0] - rows
            target[:first] = above_refs[above.index(step)][...]
            target = target.at[first:]
        target[:rows] = slabs[0][group, :, columns] * slabs[1][group, :, columns]
        if count == 3:
            target[rows:] = slabs[2][group, :, columns].astype(jnp.bfloat16)


def prepare(arrays, ranks, above=()):
    above = dict(above)
    rows, channels = arrays[0].shape
    width = channels // ranks
    out_rows = rows + sum(a.shape[0] for a in arrays[2:])
    if width % LANES:
        left, right, *below = [a.astype(jnp.float32) for a in arrays]
        packed = jnp.concatenate([left * right, *below], 0).astype(jnp.bfloat16)
        packed = packed.reshape(out_rows, ranks, width).transpose(1, 0, 2)
        device = lax.axis_index("ctx")
        pieces = [lax.dynamic_index_in_dim(packed, device ^ m, 0, False) for m in range(ranks)]
        return [jnp.concatenate([above[m], p], 0) if m in above else p for m, p in enumerate(pieces)]
    piece_rows = [out_rows + (above[m].shape[0] if m in above else 0) for m in range(ranks)]
    half = channels // 2
    slabs = [pltpu.VMEM((2, a.shape[0], half), a.dtype) for a in arrays]
    return pl.pallas_call(
        functools.partial(prepare_kernel, ranks=ranks, count=len(arrays), above=tuple(above)),
        in_specs=[pl.BlockSpec(memory_space=pltpu.HBM)] * len(arrays)
        + [pl.BlockSpec(memory_space=pltpu.VMEM)] * len(above),
        out_specs=[pl.BlockSpec(memory_space=pltpu.VMEM)] * ranks,
        out_shape=[jax.ShapeDtypeStruct((r, width), jnp.bfloat16) for r in piece_rows],
        scratch_shapes=slabs + [pltpu.SemaphoreType.DMA((2, len(arrays)))],
        compiler_params=pltpu.CompilerParams(vmem_limit_bytes=VMEM_BYTES),
        cost_estimate=pl.CostEstimate(
            flops=rows * channels, bytes_accessed=8 * out_rows * channels, transcendentals=0
        ),
    )(*(pltpu.with_memory_space_constraint(a, pltpu.HBM) for a in arrays), *above.values())


class Spans:
    def __init__(self, table_ref, slot_ref, ranks):
        self.slot_ref = slot_ref
        for slot in range(2 * ranks):
            slot_ref[table_ref[slot]] = slot

    def place(self, block):
        slot = self.slot_ref[block]
        start = pl.multiple_of(jnp.bitwise_and(slot, 1) * BLOCK, BLOCK)
        return lax.shift_right_logical(slot, 1), start

    def read(self, ref, span):
        halves = []
        for block in (2 * span, 2 * span + 1):
            source, start = self.place(block)
            halves.append(ref[source, pl.ds(start, BLOCK), :])
        return jnp.concatenate(halves, 0)

    def write(self, ref, span, values):
        for half in range(2):
            source, start = self.place(2 * span + half)
            ref[source, pl.ds(start, BLOCK), :] = values[half * BLOCK : (half + 1) * BLOCK]


def gather_pieces(pieces, recv_ref, message):
    device = lax.axis_index("ctx")
    rows = recv_ref.shape[1]
    for step, piece in zip(step_orders(len(pieces))[message], pieces):
        recv_ref[swapped(device, step)] = piece[-rows:] if message else piece[:rows]


def added(total, left, right):
    term_real = left[0] * right[0] + left[1] * right[1]
    term_imag = left[0] * right[1] - left[1] * right[0]
    return (term_real, term_imag) if total is None else (total[0] + term_real, total[1] + term_imag)


def settle(ref, index, place, sign, here, beyond):
    if beyond is not None:
        if sign > 0:
            here = here[0] + beyond[1], here[1] - beyond[0]
        else:
            here = here[0] - beyond[1], here[1] + beyond[0]
    store(ref, index, place, here)


def load(ref, index, place):
    real, imag, lanes = place
    return ref[index, real, lanes], ref[index, imag, lanes]


def store(ref, index, place, values):
    real, imag, lanes = place
    ref[index, real, lanes], ref[index, imag, lanes] = values


def each_place(width, combine):
    lane_size = LANES if width % LANES == 0 else width
    for sign in (1, -1):

        def step(index, carry, sign=sign):
            row = index * 8 if sign > 0 else index * 8 + SPAN // 2
            real = pl.ds(pl.multiple_of(row, 8), 8)
            imag = pl.ds(pl.multiple_of(row + SPAN, 8), 8)
            for lane in range(0, width, lane_size):
                combine((real, imag, slice(lane, lane + lane_size)), sign)
            return carry

        lax.fori_loop(0, SPAN // 16, step, 0)


def invert(inverse, spectrum):
    return jnp.dot(inverse, spectrum.astype(jnp.bfloat16), preferred_element_type=jnp.float32)


def weighted_kernel(table_ref, forward_ref, inverse_ref, *refs):
    slot_ref, recv_ref, f_ref, s_ref = refs[-4:]
    ranks, _, width = recv_ref.shape
    pieces, (seq_ref, w_ref, *early_refs) = refs[:ranks], refs[ranks:-4]
    spans = Spans(table_ref, slot_ref, ranks)
    gather_pieces(pieces, recv_ref, 0)
    forward = forward_ref[...]
    taps = jnp.concatenate([recv_ref[source, SPAN:, :] for source in range(ranks)], 0)
    for lag in range(LAG_SPANS):
        rows = taps[lag * SPAN : (lag + 1) * SPAN]
        f_ref[lag] = jnp.dot(forward, rows, preferred_element_type=jnp.float32)
    for span in range(ranks):
        w_ref[span] = jnp.dot(forward, spans.read(recv_ref, span), preferred_element_type=jnp.float32)

    def combine(place, sign):
        filters = [load(f_ref, lag, place) for lag in range(LAG_SPANS)]
        sums = [None] * (ranks + 1)
        for span in range(ranks):
            weighted = load(w_ref, span, place)
            for lag in range(min(LAG_SPANS - 1, span) + 1):
                sums[span - lag] = added(sums[span - lag], filters[lag], weighted)
            done = span - LAG_SPANS
            if done >= 0:
                settle(s_ref, done, place, sign, sums[done], sums[done + 1])
        for span in range(max(0, ranks - LAG_SPANS), ranks):
            settle(s_ref, span, place, sign, sums[span], sums[span + 1])

    each_place(width, combine)
    inverse = inverse_ref[...]
    for span in range(ranks):
        spans.write(seq_ref, span, invert(inverse, s_ref[span]).astype(jnp.bfloat16))
    device = lax.axis_index("ctx")
    for step, early_ref in zip(early_steps(ranks), early_refs):
        early_ref[...] = seq_ref[swapped(device, step)]


def product_kernel(table_ref, forward_ref, inverse_ref, w_ref, seq_ref, *refs):
    slot_ref, recv_ref, u_ref, g_ref = refs[-4:]
    ranks, _, width = recv_ref.shape
    pieces, targets = refs[:ranks], refs[ranks:-4]
    factor = (2.0 * BLOCK * ranks) ** -0.5
    spans = Spans(table_ref, slot_ref, ranks)
    gather_pieces(pieces, recv_ref, 1)
    forward = forward_ref[...]
    for span in range(ranks):
        u_ref[span] = jnp.dot(forward, spans.read(recv_ref, span), preferred_element_type=jnp.float32)

    def combine(place, sign):
        lagged = [None] * (LAG_SPANS + 1)
        products = []
        for span in range(ranks):
            weighted = load(w_ref, span, place)
            products.append(load(u_ref, span, place))
            for lag in range(min(LAG_SPANS, span) + 1):
                lagged[lag] = added(lagged[lag], products[span - lag], weighted)
        for lag in range(LAG_SPANS):
            settle(g_ref, lag, place, sign, lagged[lag], lagged[lag + 1])

    each_place(width, combine)
    inverse = inverse_ref[...]
    lags = [(invert(inverse, g_ref[lag]) * factor).astype(jnp.bfloat16) for lag in range(LAG_SPANS)]
    lag_rows = jnp.concatenate(lags, 0)
    taps = lag_rows.shape[0] // ranks
    device = lax.axis_index("ctx")
    for source in range(ranks):
        recv_ref[source, :taps] = lag_rows[source * taps : (source + 1) * taps]
    for step, target in enumerate(targets):
        owner = swapped(device, step)
        if step not in early_steps(ranks):
            target[:SPAN] = seq_ref[owner]
        target[-taps:] = recv_ref[owner, :taps]


def spectral_call(kernel, operands, out_shape, scratch, flops, ranks):
    whole = pl.BlockSpec(memory_space=pltpu.VMEM)
    return pl.pallas_call(
        kernel,
        in_specs=[pl.BlockSpec(memory_space=pltpu.SMEM)] + [whole] * (len(operands) - 1),
        out_specs=[whole] * len(out_shape),
        out_shape=out_shape,
        scratch_shapes=[pltpu.SMEM((2 * ranks,), jnp.int32)] + scratch,
        compiler_params=pltpu.CompilerParams(vmem_limit_bytes=VMEM_BYTES),
        cost_estimate=pl.CostEstimate(
            flops=flops,
            bytes_accessed=sum(a.size * a.dtype.itemsize for a in (*operands, *out_shape)),
            transcendentals=0,
        ),
    )(*operands)


def weighted_part(received, constants):
    ranks = len(received)
    width = received[0].shape[1]
    recv_rows = SPAN + LAG_SPANS * SPAN // ranks
    return spectral_call(
        weighted_kernel,
        (*constants, *received),
        [
            jax.ShapeDtypeStruct((ranks, SPAN, width), jnp.bfloat16),
            jax.ShapeDtypeStruct((ranks, 2 * SPAN, width), jnp.float32),
        ]
        + [jax.ShapeDtypeStruct((SPAN, width), jnp.bfloat16)] * len(early_steps(ranks)),
        [
            pltpu.VMEM((ranks, recv_rows, width), jnp.bfloat16),
            pltpu.VMEM((LAG_SPANS, 2 * SPAN, width), jnp.float32),
            pltpu.VMEM((ranks, 2 * SPAN, width), jnp.float32),
        ],
        4 * SPAN * SPAN * width * (2 * ranks + LAG_SPANS),
        ranks,
    )


def product_part(received, seq_grad, spectrum, constants):
    ranks = len(received)
    width = received[0].shape[1]
    taps = LAG_SPANS * SPAN // ranks
    early = early_steps(ranks)
    return spectral_call(
        product_kernel,
        (*constants, spectrum, seq_grad, *received),
        [
            jax.ShapeDtypeStruct((taps if step in early else SPAN + taps, width), jnp.bfloat16)
            for step in range(ranks)
        ],
        [
            pltpu.VMEM((ranks, SPAN, width), jnp.bfloat16),
            pltpu.VMEM((ranks, 2 * SPAN, width), jnp.float32),
            pltpu.VMEM((LAG_SPANS, 2 * SPAN, width), jnp.float32),
        ],
        4 * SPAN * SPAN * width * (ranks + LAG_SPANS),
        ranks,
    )


def finish_kernel(*refs, steps):
    pieces, refs = refs[: len(steps)], refs[len(steps) :]
    (key_ref, value_ref), (k_ref, v_ref, filter_ref, k_slab, v_slab, lag_slab, sems) = refs[:2], refs[-7:]
    _, rows, width = k_slab.shape
    taps = lag_slab.shape[1]
    device = lax.axis_index("ctx")
    stores = []
    for at, (step, piece) in enumerate(zip(steps, pieces)):
        columns = pl.ds(pl.multiple_of(swapped(device, step) * width, LANES), width)
        results = []
        if piece.shape[0] >= rows:
            seq_grad = piece[:rows]
            k_slab[at] = seq_grad * value_ref[:, columns]
            v_slab[at] = seq_grad * key_ref[:, columns]
            results += [(k_slab, k_ref), (v_slab, v_ref)]
        if piece.shape[0] != rows:
            lag_slab[at] = piece[-taps:].astype(jnp.float32)
            results.append((lag_slab, filter_ref))
        for sem, (slab, ref) in enumerate(results):
            stores.append(pltpu.make_async_copy(slab.at[at], ref.at[:, columns], sems.at[at, sem]))
            stores[-1].start()
    for copy in stores:
        copy.wait()


def finish_some(pieces, key_rows, value_rows, ranks, partial):
    steps = [step for step, _ in pieces]
    rows, channels = key_rows.shape
    width = channels // ranks
    taps = LAG_SPANS * SPAN // ranks
    return pl.pallas_call(
        functools.partial(finish_kernel, steps=steps),
        in_specs=[pl.BlockSpec(memory_space=pltpu.VMEM)] * (len(pieces) + 2)
        + [pl.BlockSpec(memory_space=pltpu.HBM)] * len(partial),
        out_specs=[pl.BlockSpec(memory_space=pltpu.HBM)] * 3,
        out_shape=[
            jax.ShapeDtypeStruct((rows, channels), jnp.bfloat16),
            jax.ShapeDtypeStruct((rows, channels), jnp.bfloat16),
            jax.ShapeDtypeStruct((taps, channels), jnp.float32),
        ],
        scratch_shapes=[pltpu.VMEM((len(pieces), rows, width), jnp.bfloat16)] * 2
        + [
            pltpu.VMEM((len(pieces), taps, width), jnp.float32),
            pltpu.SemaphoreType.DMA((len(pieces), 3)),
        ],
        input_output_aliases={len(pieces) + 2 + at: at for at in range(len(partial))},
        compiler_params=pltpu.CompilerParams(vmem_limit_bytes=VMEM_BYTES),
        cost_estimate=pl.CostEstimate(
            flops=2 * rows * width * len(pieces),
            bytes_accessed=width * len(pieces) * (10 * rows + 6 * taps),
            transcendentals=0,
        ),
    )(*(piece for _, piece in pieces), key_rows, value_rows, *partial)


def finish(returned, early, key_rows, value_rows):
    ranks = len(returned)
    width = returned[0].shape[1]
    rows, channels = key_rows.shape
    if width % LANES:
        pieces = [returned[step] for step in range(ranks)]
        for step, piece in early.items():
            pieces[step] = jnp.concatenate([piece, pieces[step]], 0)
        slots = swapped(lax.axis_index("ctx"), lax.iota(jnp.int32, ranks))
        flat = jnp.stack(pieces)[slots].astype(jnp.float32).transpose(1, 0, 2)
        flat = flat.reshape(-1, channels)
        seq_grad = flat[:rows]
        k_grad = (seq_grad * value_rows.astype(jnp.float32)).astype(jnp.bfloat16)
        v_grad = (seq_grad * key_rows.astype(jnp.float32)).astype(jnp.bfloat16)
        return k_grad, v_grad, flat[rows:]
    order = step_orders(ranks)[2]
    first = first_steps(ranks)
    outputs = ()
    if first:
        pieces = [(step, returned[step]) for step in order if step in first] + list(early.items())
        outputs = finish_some(pieces, key_rows, value_rows, ranks, outputs)
    pieces = [(step, returned[step]) for step in order if step not in first]
    return finish_some(pieces, key_rows, value_rows, ranks, outputs)


def on_device(out_grad, query_rows, key_rows, value_rows, conv_rows, long_filter, block_table):
    ranks = lax.axis_size("ctx")
    constants = (block_table, *(jnp.asarray(table) for table in transform_tables()))

    def swap(piece, step):
        pairs = [(rank, rank ^ step) for rank in range(ranks)]
        return lax.ppermute(piece, "ctx", pairs) if step else piece

    def exchange(pieces):
        return {step: swap(piece, step) for step, piece in pieces.items()}

    def ordered(pieces, message):
        return [pieces[step] for step in step_orders(ranks)[message]]

    joint = joint_steps(ranks)
    pieces = list(prepare((out_grad, query_rows, long_filter), ranks))
    below = list(prepare((key_rows, value_rows), ranks, {step: pieces[step] for step in joint}))
    weighted = {step: swap(below[step], step) for step in joint}
    product = dict(weighted)
    for step in range(ranks):
        if step not in joint:
            weighted[step] = swap(pieces[step], step)
            ahead = JOINT_AHEAD.get(step) if joint else None
            if ahead is not None:
                below[step], product[ahead] = lax.optimization_barrier((below[step], product[ahead]))
                weighted[ahead] = product[ahead]
            product[step] = swap(below[step], step)
    q_grad = (out_grad.astype(jnp.float32) * conv_rows.astype(jnp.float32)).astype(jnp.bfloat16)
    seq_grad, spectrum, *early = weighted_part(ordered(weighted, 0), constants)
    early = [swap(piece, step) for step, piece in zip(early_steps(ranks), early)]
    pieces = product_part(ordered(product, 1), seq_grad, spectrum, constants)
    pieces = list(pieces)
    returned = {step + ranks: piece for step, piece in zip(early_steps(ranks), early)}
    for step in step_orders(ranks)[2]:
        ahead = starts_after(ranks).get(step)
        if ahead is not None:
            pieces[step], returned[ahead] = lax.optimization_barrier((pieces[step], returned[ahead]))
        returned[step] = swap(pieces[step], step)
    early = {step: returned.pop(step + ranks) for step in early_steps(ranks)}
    return (q_grad, *finish(returned, early, key_rows, value_rows))


def solution(mesh):
    in_specs = (P("ctx", "tp"),) * 6 + (P(),)
    out_specs = (P("ctx", "tp"),) * 4
    return jax.shard_map(
        on_device, mesh=mesh, in_specs=in_specs, out_specs=out_specs, check_vma=False
    )
```

```python
import functools
import math

import jax
import jax.numpy as jnp
import ml_dtypes
import numpy as np
from jax import lax
from jax.experimental import pallas as pl
from jax.experimental.pallas import tpu as pltpu
from jax.sharding import PartitionSpec as P

BLOCK = 128
LAG_BLOCKS = 6
SPAN = 2 * BLOCK
LAG_SPANS = LAG_BLOCKS * BLOCK // SPAN
LANES = 128
GROUPS = 4
VMEM_BYTES = 32 * 2**20


def step_orders(ranks):
    if ranks != 8:
        return [list(range(ranks))] * 3
    return [4, 2, 6, 7, 5, 3, 1, 0], [5, 3, 1, 2, 6, 7, 4, 0], [4, 2, 5, 3, 1, 6, 7, 0]


def joint_steps(ranks):
    return [5, 3, 1] if ranks == 8 else []


def early_steps(ranks):
    return [6, 7] if ranks == 8 else []


def first_steps(ranks):
    return [0, 2, 4] if ranks == 8 else []


def starts_after(ranks):
    return {4: 8 + 6, 2: 8 + 7, 1: 2, 6: 2, 7: 2} if ranks == 8 else {}


def transform_tables():
    order = np.concatenate([np.arange(0, SPAN, 2), np.arange(1, SPAN, 2)])
    angles = np.outer(order + 0.5, np.arange(SPAN)) * (math.pi / SPAN)
    forward = np.concatenate([np.cos(angles), -np.sin(angles)], 0)
    inverse = forward.T / SPAN
    return forward.astype(ml_dtypes.bfloat16), inverse.astype(ml_dtypes.bfloat16)


def swapped(device, step):
    return jnp.bitwise_xor(device, step)


def prepare_kernel(*refs, ranks, count, above):
    sources, above_refs, refs = refs[:count], refs[count : count + len(above)], refs[count + len(above) :]
    targets, rest = refs[:ranks], refs[ranks:]
    slabs, in_sems = rest[:count], rest[count]
    groups, rows, total = slabs[0].shape
    owners = ranks // groups
    width = total // owners
    device = lax.axis_index("ctx")
    upper = lax.shift_right_logical(device, int(math.log2(owners)))
    loads = []
    for group in range(groups):
        columns = pl.ds(pl.multiple_of(swapped(upper, group) * total, LANES), total)
        loads.append(
            [
                pltpu.make_async_copy(source.at[:, columns], slab.at[group], in_sems.at[group, at])
                for at, (source, slab) in enumerate(zip(sources, slabs))
            ]
        )
        for load in loads[group]:
            load.start()
    for step in range(ranks):
        group, inner = divmod(step, owners)
        if inner == 0:
            for load in loads[group]:
                load.wait()
        column = jnp.bitwise_and(swapped(device, inner), owners - 1) * width
        columns = pl.ds(pl.multiple_of(column, LANES), width)
        target = targets[step]
        if step in above:
            first = target.shape[0] - rows
            target[:first] = above_refs[above.index(step)][...]
            target = target.at[first:]
        target[:rows] = slabs[0][group, :, columns] * slabs[1][group, :, columns]
        if count == 3:
            target[rows:] = slabs[2][group, :, columns].astype(jnp.bfloat16)


def prepare(arrays, ranks, above=()):
    above = dict(above)
    rows, channels = arrays[0].shape
    width = channels // ranks
    out_rows = rows + sum(a.shape[0] for a in arrays[2:])
    if width % LANES:
        left, right, *below = [a.astype(jnp.float32) for a in arrays]
        packed = jnp.concatenate([left * right, *below], 0).astype(jnp.bfloat16)
        packed = packed.reshape(out_rows, ranks, width).transpose(1, 0, 2)
        device = lax.axis_index("ctx")
        pieces = [lax.dynamic_index_in_dim(packed, device ^ m, 0, False) for m in range(ranks)]
        return [jnp.concatenate([above[m], p], 0) if m in above else p for m, p in enumerate(pieces)]
    piece_rows = [out_rows + (above[m].shape[0] if m in above else 0) for m in range(ranks)]
    slabs = [pltpu.VMEM((GROUPS, a.shape[0], channels // GROUPS), a.dtype) for a in arrays]
    return pl.pallas_call(
        functools.partial(prepare_kernel, ranks=ranks, count=len(arrays), above=tuple(above)),
        in_specs=[pl.BlockSpec(memory_space=pltpu.HBM)] * len(arrays)
        + [pl.BlockSpec(memory_space=pltpu.VMEM)] * len(above),
        out_specs=[pl.BlockSpec(memory_space=pltpu.VMEM)] * ranks,
        out_shape=[jax.ShapeDtypeStruct((r, width), jnp.bfloat16) for r in piece_rows],
        scratch_shapes=slabs + [pltpu.SemaphoreType.DMA((GROUPS, len(arrays)))],
        compiler_params=pltpu.CompilerParams(vmem_limit_bytes=VMEM_BYTES),
        cost_estimate=pl.CostEstimate(
            flops=rows * channels, bytes_accessed=8 * out_rows * channels, transcendentals=0
        ),
    )(*(pltpu.with_memory_space_constraint(a, pltpu.HBM) for a in arrays), *above.values())


class Spans:
    def __init__(self, table_ref, slot_ref, ranks):
        self.slot_ref = slot_ref
        for slot in range(2 * ranks):
            slot_ref[table_ref[slot]] = slot

    def place(self, block):
        slot = self.slot_ref[block]
        start = pl.multiple_of(jnp.bitwise_and(slot, 1) * BLOCK, BLOCK)
        return lax.shift_right_logical(slot, 1), start

    def read(self, ref, span):
        halves = []
        for block in (2 * span, 2 * span + 1):
            source, start = self.place(block)
            halves.append(ref[source, pl.ds(start, BLOCK), :])
        return jnp.concatenate(halves, 0)

    def write(self, ref, span, values):
        for half in range(2):
            source, start = self.place(2 * span + half)
            ref[source, pl.ds(start, BLOCK), :] = values[half * BLOCK : (half + 1) * BLOCK]


def gather_pieces(pieces, recv_ref, message):
    device = lax.axis_index("ctx")
    rows = recv_ref.shape[1]
    for step, piece in zip(step_orders(len(pieces))[message], pieces):
        recv_ref[swapped(device, step)] = piece[-rows:] if message else piece[:rows]


def added(total, left, right):
    term_real = left[0] * right[0] + left[1] * right[1]
    term_imag = left[0] * right[1] - left[1] * right[0]
    return (term_real, term_imag) if total is None else (total[0] + term_real, total[1] + term_imag)


def settle(ref, index, place, sign, here, beyond):
    if beyond is not None:
        if sign > 0:
            here = here[0] + beyond[1], here[1] - beyond[0]
        else:
            here = here[0] - beyond[1], here[1] + beyond[0]
    store(ref, index, place, here)


def load(ref, index, place):
    real, imag, lanes = place
    return ref[index, real, lanes], ref[index, imag, lanes]


def store(ref, index, place, values):
    real, imag, lanes = place
    ref[index, real, lanes], ref[index, imag, lanes] = values


def each_place(width, combine):
    lane_size = LANES if width % LANES == 0 else width
    for sign in (1, -1):

        def step(index, carry, sign=sign):
            row = index * 8 if sign > 0 else index * 8 + SPAN // 2
            real = pl.ds(pl.multiple_of(row, 8), 8)
            imag = pl.ds(pl.multiple_of(row + SPAN, 8), 8)
            for lane in range(0, width, lane_size):
                combine((real, imag, slice(lane, lane + lane_size)), sign)
            return carry

        lax.fori_loop(0, SPAN // 16, step, 0)


def invert(inverse, spectrum):
    return jnp.dot(inverse, spectrum.astype(jnp.bfloat16), preferred_element_type=jnp.float32)


def weighted_kernel(table_ref, forward_ref, inverse_ref, *refs):
    slot_ref, recv_ref, f_ref, s_ref = refs[-4:]
    ranks, _, width = recv_ref.shape
    pieces, (seq_ref, w_ref, *early_refs) = refs[:ranks], refs[ranks:-4]
    spans = Spans(table_ref, slot_ref, ranks)
    gather_pieces(pieces, recv_ref, 0)
    forward = forward_ref[...]
    taps = jnp.concatenate([recv_ref[source, SPAN:, :] for source in range(ranks)], 0)
    for lag in range(LAG_SPANS):
        rows = taps[lag * SPAN : (lag + 1) * SPAN]
        f_ref[lag] = jnp.dot(forward, rows, preferred_element_type=jnp.float32)
    for span in range(ranks):
        w_ref[span] = jnp.dot(forward, spans.read(recv_ref, span), preferred_element_type=jnp.float32)

    def combine(place, sign):
        filters = [load(f_ref, lag, place) for lag in range(LAG_SPANS)]
        sums = [None] * (ranks + 1)
        for span in range(ranks):
            weighted = load(w_ref, span, place)
            for lag in range(min(LAG_SPANS - 1, span) + 1):
                sums[span - lag] = added(sums[span - lag], filters[lag], weighted)
            done = span - LAG_SPANS
            if done >= 0:
                settle(s_ref, done, place, sign, sums[done], sums[done + 1])
        for span in range(max(0, ranks - LAG_SPANS), ranks):
            settle(s_ref, span, place, sign, sums[span], sums[span + 1])

    each_place(width, combine)
    inverse = inverse_ref[...]
    for span in range(ranks):
        spans.write(seq_ref, span, invert(inverse, s_ref[span]).astype(jnp.bfloat16))
    device = lax.axis_index("ctx")
    for step, early_ref in zip(early_steps(ranks), early_refs):
        early_ref[...] = seq_ref[swapped(device, step)]


def product_kernel(table_ref, forward_ref, inverse_ref, w_ref, seq_ref, *refs):
    slot_ref, recv_ref, u_ref, g_ref = refs[-4:]
    ranks, _, width = recv_ref.shape
    pieces, targets = refs[:ranks], refs[ranks:-4]
    factor = (2.0 * BLOCK * ranks) ** -0.5
    spans = Spans(table_ref, slot_ref, ranks)
    gather_pieces(pieces, recv_ref, 1)
    forward = forward_ref[...]
    for span in range(ranks):
        u_ref[span] = jnp.dot(forward, spans.read(recv_ref, span), preferred_element_type=jnp.float32)

    def combine(place, sign):
        lagged = [None] * (LAG_SPANS + 1)
        products = []
        for span in range(ranks):
            weighted = load(w_ref, span, place)
            products.append(load(u_ref, span, place))
            for lag in range(min(LAG_SPANS, span) + 1):
                lagged[lag] = added(lagged[lag], products[span - lag], weighted)
        for lag in range(LAG_SPANS):
            settle(g_ref, lag, place, sign, lagged[lag], lagged[lag + 1])

    each_place(width, combine)
    inverse = inverse_ref[...]
    lags = [(invert(inverse, g_ref[lag]) * factor).astype(jnp.bfloat16) for lag in range(LAG_SPANS)]
    lag_rows = jnp.concatenate(lags, 0)
    taps = lag_rows.shape[0] // ranks
    device = lax.axis_index("ctx")
    for source in range(ranks):
        recv_ref[source, :taps] = lag_rows[source * taps : (source + 1) * taps]
    for step, target in enumerate(targets):
        owner = swapped(device, step)
        if step not in early_steps(ranks):
            target[:SPAN] = seq_ref[owner]
        target[-taps:] = recv_ref[owner, :taps]


def spectral_call(kernel, operands, out_shape, scratch, flops, ranks):
    whole = pl.BlockSpec(memory_space=pltpu.VMEM)
    return pl.pallas_call(
        kernel,
        in_specs=[pl.BlockSpec(memory_space=pltpu.SMEM)] + [whole] * (len(operands) - 1),
        out_specs=[whole] * len(out_shape),
        out_shape=out_shape,
        scratch_shapes=[pltpu.SMEM((2 * ranks,), jnp.int32)] + scratch,
        compiler_params=pltpu.CompilerParams(vmem_limit_bytes=VMEM_BYTES),
        cost_estimate=pl.CostEstimate(
            flops=flops,
            bytes_accessed=sum(a.size * a.dtype.itemsize for a in (*operands, *out_shape)),
            transcendentals=0,
        ),
    )(*operands)


def weighted_part(received, constants):
    ranks = len(received)
    width = received[0].shape[1]
    recv_rows = SPAN + LAG_SPANS * SPAN // ranks
    return spectral_call(
        weighted_kernel,
        (*constants, *received),
        [
            jax.ShapeDtypeStruct((ranks, SPAN, width), jnp.bfloat16),
            jax.ShapeDtypeStruct((ranks, 2 * SPAN, width), jnp.float32),
        ]
        + [jax.ShapeDtypeStruct((SPAN, width), jnp.bfloat16)] * len(early_steps(ranks)),
        [
            pltpu.VMEM((ranks, recv_rows, width), jnp.bfloat16),
            pltpu.VMEM((LAG_SPANS, 2 * SPAN, width), jnp.float32),
            pltpu.VMEM((ranks, 2 * SPAN, width), jnp.float32),
        ],
        4 * SPAN * SPAN * width * (2 * ranks + LAG_SPANS),
        ranks,
    )


def product_part(received, seq_grad, spectrum, constants):
    ranks = len(received)
    width = received[0].shape[1]
    taps = LAG_SPANS * SPAN // ranks
    early = early_steps(ranks)
    return spectral_call(
        product_kernel,
        (*constants, spectrum, seq_grad, *received),
        [
            jax.ShapeDtypeStruct((taps if step in early else SPAN + taps, width), jnp.bfloat16)
            for step in range(ranks)
        ],
        [
            pltpu.VMEM((ranks, SPAN, width), jnp.bfloat16),
            pltpu.VMEM((ranks, 2 * SPAN, width), jnp.float32),
            pltpu.VMEM((LAG_SPANS, 2 * SPAN, width), jnp.float32),
        ],
        4 * SPAN * SPAN * width * (ranks + LAG_SPANS),
        ranks,
    )


def finish_kernel(*refs, steps):
    pieces, refs = refs[: len(steps)], refs[len(steps) :]
    (key_ref, value_ref), (k_ref, v_ref, filter_ref, k_slab, v_slab, lag_slab, sems) = refs[:2], refs[-7:]
    _, rows, width = k_slab.shape
    taps = lag_slab.shape[1]
    device = lax.axis_index("ctx")
    stores = []
    for at, (step, piece) in enumerate(zip(steps, pieces)):
        columns = pl.ds(pl.multiple_of(swapped(device, step) * width, LANES), width)
        results = []
        if piece.shape[0] >= rows:
            seq_grad = piece[:rows]
            k_slab[at] = seq_grad * value_ref[:, columns]
            v_slab[at] = seq_grad * key_ref[:, columns]
            results += [(k_slab, k_ref), (v_slab, v_ref)]
        if piece.shape[0] != rows:
            lag_slab[at] = piece[-taps:].astype(jnp.float32)
            results.append((lag_slab, filter_ref))
        for sem, (slab, ref) in enumerate(results):
            stores.append(pltpu.make_async_copy(slab.at[at], ref.at[:, columns], sems.at[at, sem]))
            stores[-1].start()
    for copy in stores:
        copy.wait()


def finish_some(pieces, key_rows, value_rows, ranks, partial):
    steps = [step for step, _ in pieces]
    rows, channels = key_rows.shape
    width = channels // ranks
    taps = LAG_SPANS * SPAN // ranks
    return pl.pallas_call(
        functools.partial(finish_kernel, steps=steps),
        in_specs=[pl.BlockSpec(memory_space=pltpu.VMEM)] * (len(pieces) + 2)
        + [pl.BlockSpec(memory_space=pltpu.HBM)] * len(partial),
        out_specs=[pl.BlockSpec(memory_space=pltpu.HBM)] * 3,
        out_shape=[
            jax.ShapeDtypeStruct((rows, channels), jnp.bfloat16),
            jax.ShapeDtypeStruct((rows, channels), jnp.bfloat16),
            jax.ShapeDtypeStruct((taps, channels), jnp.float32),
        ],
        scratch_shapes=[pltpu.VMEM((len(pieces), rows, width), jnp.bfloat16)] * 2
        + [
            pltpu.VMEM((len(pieces), taps, width), jnp.float32),
            pltpu.SemaphoreType.DMA((len(pieces), 3)),
        ],
        input_output_aliases={len(pieces) + 2 + at: at for at in range(len(partial))},
        compiler_params=pltpu.CompilerParams(vmem_limit_bytes=VMEM_BYTES),
        cost_estimate=pl.CostEstimate(
            flops=2 * rows * width * len(pieces),
            bytes_accessed=width * len(pieces) * (10 * rows + 6 * taps),
            transcendentals=0,
        ),
    )(*(piece for _, piece in pieces), key_rows, value_rows, *partial)


def finish(returned, early, key_rows, value_rows):
    ranks = len(returned)
    width = returned[0].shape[1]
    rows, channels = key_rows.shape
    if width % LANES:
        pieces = [returned[step] for step in range(ranks)]
        for step, piece in early.items():
            pieces[step] = jnp.concatenate([piece, pieces[step]], 0)
        slots = swapped(lax.axis_index("ctx"), lax.iota(jnp.int32, ranks))
        flat = jnp.stack(pieces)[slots].astype(jnp.float32).transpose(1, 0, 2)
        flat = flat.reshape(-1, channels)
        seq_grad = flat[:rows]
        k_grad = (seq_grad * value_rows.astype(jnp.float32)).astype(jnp.bfloat16)
        v_grad = (seq_grad * key_rows.astype(jnp.float32)).astype(jnp.bfloat16)
        return k_grad, v_grad, flat[rows:]
    order = step_orders(ranks)[2]
    first = first_steps(ranks)
    outputs = ()
    if first:
        pieces = [(step, returned[step]) for step in order if step in first] + list(early.items())
        outputs = finish_some(pieces, key_rows, value_rows, ranks, outputs)
    pieces = [(step, returned[step]) for step in order if step not in first]
    return finish_some(pieces, key_rows, value_rows, ranks, outputs)


def on_device(out_grad, query_rows, key_rows, value_rows, conv_rows, long_filter, block_table):
    ranks = lax.axis_size("ctx")
    constants = (block_table, *(jnp.asarray(table) for table in transform_tables()))

    def swap(piece, step):
        pairs = [(rank, rank ^ step) for rank in range(ranks)]
        return lax.ppermute(piece, "ctx", pairs) if step else piece

    def exchange(pieces):
        return {step: swap(piece, step) for step, piece in pieces.items()}

    def ordered(pieces, message):
        return [pieces[step] for step in step_orders(ranks)[message]]

    joint = joint_steps(ranks)
    pieces = prepare((out_grad, query_rows, long_filter), ranks)
    weighted = exchange({step: pieces[step] for step in range(ranks) if step not in joint})
    pieces = prepare((key_rows, value_rows), ranks, {step: pieces[step] for step in joint})
    product = exchange(dict(enumerate(pieces)))
    weighted |= {step: product[step] for step in joint}
    q_grad = (out_grad.astype(jnp.float32) * conv_rows.astype(jnp.float32)).astype(jnp.bfloat16)
    seq_grad, spectrum, *early = weighted_part(ordered(weighted, 0), constants)
    early = [swap(piece, step) for step, piece in zip(early_steps(ranks), early)]
    pieces = product_part(ordered(product, 1), seq_grad, spectrum, constants)
    pieces = list(pieces)
    returned = {step + ranks: piece for step, piece in zip(early_steps(ranks), early)}
    for step in step_orders(ranks)[2]:
        ahead = starts_after(ranks).get(step)
        if ahead is not None:
            pieces[step], returned[ahead] = lax.optimization_barrier((pieces[step], returned[ahead]))
        returned[step] = swap(pieces[step], step)
    early = {step: returned.pop(step + ranks) for step in early_steps(ranks)}
    return (q_grad, *finish(returned, early, key_rows, value_rows))


def solution(mesh):
    in_specs = (P("ctx", "tp"),) * 6 + (P(),)
    out_specs = (P("ctx", "tp"),) * 4
    return jax.shard_map(
        on_device, mesh=mesh, in_specs=in_specs, out_specs=out_specs, check_vma=False
    )
```
